256 devices in a mesh: dp: 16 (over y_hi, z), tensor: 16 (over x, y_lo, core).
Axes of the slice: x: 4, y: 4 (y_hi: 2, y_lo: 2; y = y_hi * 2 + y_lo), z: 8, core: 2. Of those that a mesh axis runs over, the one named last changes fastest.
Arguments:
- out_grad: bfloat16 [8192, 2048], P('dp'), may hold values from -6 to 6
- down_weight: bfloat16 [11008, 2048], P('tensor'), may hold values from -0.125 to 0.125
- gate_pre: bfloat16 [8192, 11008], P('dp', 'tensor'), may hold values from -8 to 8
Outputs:
- factor: float32 [11008, 11008], P('dp', 'tensor')
The draws below stay inside these ranges and needn't reach their ends.
All inputs are finite; a program needn't handle non-finite values.
Results may differ from the reference program's by a relative error of at most 0.014.
Values may be sent and summed in bfloat16 or wider, within the bound.
No kernel may reach another device: no remote copies, remote signals or barrier semaphores. Data moves between devices by JAX's collectives and lax.ppermute only.
A program may use at most 128 MiB of HBM per device.

```python
import jax
import jax.numpy as jnp
from jax import lax

D = 2048
FF = 11008
TOKENS = 8192


def raised(values, stream_key, source, target, shards_of, factor):
    def block_of(position):
        return (jnp.arange(values.shape[position]) // (values.shape[position] // shards_of)).reshape((-1,) + (1,) * (values.ndim - 1 - position))

    near = jax.random.permutation(stream_key, shards_of)[block_of(target)]
    second = (block_of(target) + shards_of // 2) % shards_of
    return jnp.where((block_of(source) == near) | (block_of(source) == second), factor * values, values)


def levels(rng, extent, split, smallest, high):
    gain = 1.0
    for position, parts in split:
        draws = jax.random.uniform(jax.random.fold_in(jax.random.fold_in(rng, 6), position), (parts,), jnp.float32, smallest / len(split), high / len(split))
        gain = gain * jnp.repeat(jnp.exp(draws), extent[position] // parts).reshape((-1,) + (1,) * (len(extent) - 1 - position))
    return gain


def centred(key, shape, deviation, bound, cuts=(), held_as=jnp.bfloat16):
    drawn = jax.random.normal(key, shape, jnp.float32) * deviation
    if len(cuts) > 0:
        drawn = levels(key, shape, cuts, -0.22, 0.18) * drawn
    return jnp.clip(drawn, min=-bound, max=bound).astype(held_as)


def heavy_noise(key, shape, spread, most, cuts, heavy, kind=jnp.bfloat16):
    drawn = spread * jax.random.normal(key, shape, jnp.float32)
    if cuts:
        drawn = drawn * levels(key, shape, cuts, -0.22, 0.18)
    return jnp.clip(raised(drawn, jax.random.fold_in(key, 3), *heavy), -most, most).astype(kind)


def setup_inputs(seed: int = 0) -> dict:
    splits = jax.random.split(jax.random.key(seed), 4)
    return {
        "out_grad": centred(splits[0], (TOKENS, D), 1.0, 6.0, ((0, 16),)),
        "down_weight": centred(splits[1], (FF, D), D ** -0.5, 0.125, ((0, 16),)),
        "gate_pre": heavy_noise(splits[2], (TOKENS, FF), 1.5, 8.0, ((0, 16), (1, 16)), (0, 1, 16, 2.0)),
    }


def reference(out_grad, down_weight, gate_pre):
    hidden_grad = lax.dot_general(out_grad, down_weight, (((1,), (1,)), ((), ())), preferred_element_type=jnp.float32).astype(jnp.bfloat16)
    up_grad = (hidden_grad.astype(jnp.float32) * jax.nn.silu(gate_pre.astype(jnp.float32))).astype(jnp.bfloat16)
    summed = lax.dot_general(up_grad, up_grad, (((0,), (0,)), ((), ())), preferred_element_type=jnp.float32)
    return summed / jnp.float32(TOKENS)
```

```python
import jax
import jax.numpy as jnp
from jax import lax
from jax.experimental import pallas as pl
from jax.experimental.pallas import tpu as pltpu
from jax.sharding import PartitionSpec as P

BOTH = ("dp", "tensor")
RING = 8
PLACES = (0, 4, 1, 7, 2, 6, 3, 5)


def place(offset, half):
    k = PLACES.index(offset)
    return (k // 2) * 4 + half * 2 + k % 2


def spread(turn):
    pairs = []
    for h in range(2):
        for source in range(RING):
            for b in range(2):
                for z in range(RING):
                    target = (h * RING + z) * 16 + place((source - z) % RING, b ^ turn)
                    pairs.append(((h * RING + source) * 16 + b * RING + z, target))
    return pairs


def along_z(step):
    return [(h * RING + z, h * RING + (z + step) % RING) for h in range(2) for z in range(RING)]


ACROSS = [(i, (i + RING) % 16) for i in range(16)]


def product_body(rows_ref, columns_ref, out_ref, total):
    k = pl.program_id(0)

    @pl.when(k == 0)
    def _():
        total[...] = jnp.zeros_like(total)

    for half in range(2):
        total[half] += lax.dot_general(
            rows_ref[0, half, 0], columns_ref[0], (((1,), (1,)), ((), ())),
            preferred_element_type=jnp.float32,
        )

    @pl.when(k == RING - 1)
    def _():
        out_ref[...] = total[...].astype(out_ref.dtype)


def finish_body(rows_ref, columns_ref, other_ref, out_ref, total, *, scale):
    k = pl.program_id(0)

    @pl.when(k == 0)
    def _():
        total[...] = other_ref[...].astype(jnp.float32)

    for half in range(2):
        total[half] += lax.dot_general(
            rows_ref[0, half, 0], columns_ref[0], (((1,), (1,)), ((), ())),
            preferred_element_type=jnp.float32,
        )

    @pl.when(k == RING - 1)
    def _():
        out_ref[...] = total[...] * scale


def product(rows, columns, other=None, scale=None):
    part, tokens = rows.shape[3:]
    n = columns.shape[1]
    in_specs = [
        pl.BlockSpec((1, 2, 1, part, tokens), lambda k: (k // 2, 0, k % 2, 0, 0)),
        pl.BlockSpec((1, n, tokens), lambda k: (k, 0, 0)),
    ]
    whole = pl.BlockSpec((2, part, n), lambda k: (0, 0, 0))
    args = [rows, columns]
    if other is None:
        body, kind = product_body, jnp.bfloat16
    else:
        def body(*refs):
            finish_body(*refs, scale=scale)
        kind = jnp.float32
        in_specs.append(whole)
        args.append(other)
    return pl.pallas_call(
        body,
        grid=(RING,),
        in_specs=in_specs,
        out_specs=whole,
        out_shape=jax.ShapeDtypeStruct((2, part, n), kind),
        scratch_shapes=[pltpu.VMEM((2, part, n), jnp.float32)],
        compiler_params=pltpu.CompilerParams(
            dimension_semantics=("arbitrary",), vmem_limit_bytes=32 * 1024 * 1024
        ),
        cost_estimate=pl.CostEstimate(
            flops=2 * 2 * part * n * tokens * RING, bytes_accessed=16 * 1024 * 1024, transcendentals=0
        ),
    )(*args)


def shards(out_grad, down_weight, gate_pre):
    n, tokens = down_weight.shape[0], out_grad.shape[0]
    part = n // 2
    hidden_grad = lax.dot_general(
        down_weight, out_grad, (((1,), (1,)), ((), ())), preferred_element_type=jnp.float32
    ).astype(jnp.bfloat16)
    up_grad = (hidden_grad.astype(jnp.float32) * jax.nn.silu(gate_pre.T.astype(jnp.float32))).astype(
        jnp.bfloat16
    )
    h = lax.axis_index("dp") // RING
    t = lax.axis_index("tensor")
    b, half = t // RING, (t // 2) % 2

    low, high = up_grad[:part], up_grad[part:]
    got = [
        lax.ppermute(jnp.where((b ^ turn) == 0, low, high), BOTH, spread(turn)) for turn in range(2)
    ]
    first_turn = half ^ (1 - h)
    theirs = jnp.where(first_turn == 0, got[0], got[1])
    ours = jnp.where(first_turn == 0, got[1], got[0])

    blocks = {0: up_grad}
    up, down = up_grad, up_grad
    for step in range(1, RING // 2):
        up = lax.ppermute(up, "dp", along_z(1))
        down = lax.ppermute(down, "dp", along_z(-1))
        blocks[RING - step], blocks[step] = up, down
    blocks[RING // 2] = jnp.concatenate(
        [lax.ppermute(up[:part], "dp", along_z(1)), lax.ppermute(down[part:], "dp", along_z(-1))], axis=0
    )
    columns = jnp.stack([blocks[offset] for offset in PLACES])

    rows_theirs = lax.all_gather(theirs, "tensor", axis=0).reshape(4, 2, 2, part, tokens)
    rows_ours = lax.all_gather(ours, "tensor", axis=0).reshape(4, 2, 2, part, tokens)
    sent = lax.ppermute(product(rows_theirs, columns), "dp", ACROSS)
    total = tokens * lax.axis_size("dp")
    return product(rows_ours, columns, sent, 1.0 / total).reshape(n, n)


def solution(mesh):
    placed = (P("dp", None), P("tensor", None), P("dp", "tensor"))
    return jax.shard_map(
        shards, mesh=mesh, in_specs=placed, out_specs=P("dp", "tensor"), check_vma=False
    )
```

```python
import functools

import jax
import jax.numpy as jnp
from jax import lax
from jax.experimental import pallas as pl
from jax.experimental.pallas import tpu as pltpu
from jax.sharding import PartitionSpec as P

BOTH = ("dp", "tensor")
RING = 8
PLACES = (0, 4, 1, 7, 2, 6, 3, 5)


def place(offset, half):
    k = PLACES.index(offset)
    return (k // 2) * 4 + half * 2 + k % 2


def in_plane(turn):
    pairs = []
    for h in range(2):
        for source in range(RING):
            for b in range(2):
                for z in range(RING):
                    plane = (h * RING + source) * 16
                    pairs.append((plane + b * RING + z, plane + place((source - z) % RING, b ^ turn)))
    return pairs


def shifted():
    pairs = []
    for h in range(2):
        for z in range(RING):
            for offset in range(RING):
                for half in range(2):
                    t = place(offset, half)
                    pairs.append(((h * RING + (z + offset) % RING) * 16 + t, (h * RING + z) * 16 + t))
    return pairs


def along_z(step):
    return [(h * RING + z, h * RING + (z + step) % RING) for h in range(2) for z in range(RING)]


ACROSS = [(i, (i + RING) % 16) for i in range(16)]


def product_body(rows_ref, columns_ref, *refs, steps, scale):
    out_ref, total = refs[-2:]
    k = pl.program_id(0)
    pair = columns_ref.shape[0]

    def partial(half):
        return sum(
            lax.dot_general(
                rows_ref[0, half, i], columns_ref[i], (((1,), (1,)), ((), ())),
                preferred_element_type=jnp.float32,
            )
            for i in range(pair)
        )

    @pl.when(k == 0)
    def _():
        for half in range(2):
            total[half] = partial(half)

    @pl.when((k > 0) & (k < steps - 1))
    def _():
        for half in range(2):
            total[half] += partial(half)

    @pl.when(k == steps - 1)
    def _():
        for half in range(2):
            whole = total[half] + partial(half)
            if scale is not None:
                whole = (whole + refs[0][half].astype(jnp.float32)) * scale
            out_ref[half] = whole.astype(out_ref.dtype)


def product(rows, columns, other=None, scale=None):
    steps, part, tokens = rows.shape[0], *rows.shape[3:]
    n = columns.shape[1]
    in_specs = [
        pl.BlockSpec((1, 2, 2, part, tokens), lambda k: (k, 0, 0, 0, 0)),
        pl.BlockSpec((2, n, tokens), lambda k: (k, 0, 0)),
    ]
    whole = pl.BlockSpec((2, part, n), lambda k: (0, 0, 0))
    args = [rows, columns]
    if other is not None:
        in_specs.append(whole)
        args.append(other)
    return pl.pallas_call(
        functools.partial(product_body, steps=steps, scale=scale),
        grid=(steps,),
        in_specs=in_specs,
        out_specs=whole,
        out_shape=jax.ShapeDtypeStruct((2, part, n), jnp.bfloat16 if other is None else jnp.float32),
        scratch_shapes=[pltpu.VMEM((2, part, n), jnp.float32)],
        compiler_params=pltpu.CompilerParams(
            dimension_semantics=("arbitrary",), vmem_limit_bytes=56 * 1024 * 1024
        ),
        cost_estimate=pl.CostEstimate(
            flops=2 * 2 * part * n * tokens * RING, bytes_accessed=16 * 1024 * 1024, transcendentals=0
        ),
    )(*args)


def put(columns, block, offset, start=0):
    return lax.dynamic_update_slice(columns, block[None], (PLACES.index(offset), start, 0))


def shards(out_grad, down_weight, gate_pre):
    n, tokens = down_weight.shape[0], out_grad.shape[0]
    part = n // 2
    hidden_grad = lax.dot_general(
        down_weight, out_grad, (((1,), (1,)), ((), ())), preferred_element_type=jnp.float32
    ).astype(jnp.bfloat16)
    up_grad = (hidden_grad.astype(jnp.float32) * jax.nn.silu(gate_pre.T.astype(jnp.float32))).astype(
        jnp.bfloat16
    )
    h = lax.axis_index("dp") // RING
    t = lax.axis_index("tensor")
    b, half = t // RING, (t // 2) % 2

    low, high = up_grad[:part], up_grad[part:]
    got = [
        lax.ppermute(jnp.where((b ^ turn) == 0, low, high), BOTH, in_plane(turn)) for turn in range(2)
    ]
    up, down = lax.ppermute(up_grad, "dp", along_z(1)), lax.ppermute(up_grad, "dp", along_z(-1))
    got[0], got[1], up, down, up_grad = lax.optimization_barrier((got[0], got[1], up, down, up_grad))

    first_turn = half ^ (1 - h)
    theirs = jnp.where(first_turn == 0, got[0], got[1])
    ours = jnp.where(first_turn == 0, got[1], got[0])
    theirs = lax.ppermute(theirs, BOTH, shifted())
    columns = jnp.broadcast_to(up_grad[None], (RING, n, tokens))
    columns = put(put(columns, up, RING - 1), down, 1)
    theirs, up, down, ours, columns = lax.optimization_barrier((theirs, up, down, ours, columns))
    rows_theirs = lax.all_gather(theirs, "tensor", axis=0).reshape(4, 2, 2, part, tokens)

    up, down = lax.ppermute(up, "dp", along_z(1)), lax.ppermute(down, "dp", along_z(-1))
    ours = lax.ppermute(ours, BOTH, shifted())
    up, down, ours, columns = lax.optimization_barrier((up, down, ours, columns))
    rows_ours = lax.all_gather(ours, "tensor", axis=0).reshape(4, 2, 2, part, tokens)

    columns = put(put(columns, up, RING - 2), down, 2)
    up, down = lax.ppermute(up, "dp", along_z(1)), lax.ppermute(down, "dp", along_z(-1))
    up, down, columns = lax.optimization_barrier((up, down, columns))

    columns = put(put(columns, up, RING - 3), down, 3)
    up = lax.ppermute(up[:part], "dp", along_z(1))
    down = lax.ppermute(down[part:], "dp", along_z(-1))
    up, down, columns = lax.optimization_barrier((up, down, columns))
    columns = put(put(columns, up, RING // 2), down, RING // 2, part)
    sent = lax.ppermute(product(rows_theirs, columns), "dp", ACROSS)
    total = tokens * lax.axis_size("dp")
    return product(rows_ours, columns, sent, 1.0 / total).reshape(n, n)


def solution(mesh):
    placed = (P("dp", None), P("tensor", None), P("dp", "tensor"))
    return jax.shard_map(
        shards, mesh=mesh, in_specs=placed, out_specs=P("dp", "tensor"), check_vma=False
    )
```

```python
import functools

import jax
import jax.numpy as jnp
from jax import lax
from jax.experimental import pallas as pl
from jax.experimental.pallas import tpu as pltpu
from jax.sharding import PartitionSpec as P

BOTH = ("dp", "tensor")
RING = 8
PLACES = (0, 4, 1, 7, 2, 6, 3, 5)


def place(offset, half):
    k = PLACES.index(offset)
    return (k // 2) * 4 + half * 2 + k % 2


def in_plane(turn):
    pairs = []
    for h in range(2):
        for source in range(RING):
            for b in range(2):
                for z in range(RING):
                    plane = (h * RING + source) * 16
                    pairs.append((plane + b * RING + z, plane + place((source - z) % RING, b ^ turn)))
    return pairs


def shifted():
    pairs = []
    for h in range(2):
        for z in range(RING):
            for offset in range(RING):
                for half in range(2):
                    t = place(offset, half)
                    pairs.append(((h * RING + (z + offset) % RING) * 16 + t, (h * RING + z) * 16 + t))
    return pairs


def along_z(step):
    return [(h * RING + z, h * RING + (z + step) % RING) for h in range(2) for z in range(RING)]


ACROSS = [(i, (i + RING) % 16) for i in range(16)]


def product_body(rows_ref, columns_ref, out_ref, total, *, steps):
    k = pl.program_id(0)
    pair = columns_ref.shape[0]

    def partial(half):
        return sum(
            lax.dot_general(
                rows_ref[0, half, i], columns_ref[i], (((1,), (1,)), ((), ())),
                preferred_element_type=jnp.float32,
            )
            for i in range(pair)
        )

    @pl.when(k == 0)
    def _():
        for half in range(2):
            total[half] = partial(half)

    @pl.when((k > 0) & (k < steps - 1))
    def _():
        for half in range(2):
            total[half] += partial(half)

    @pl.when(k == steps - 1)
    def _():
        for half in range(2):
            out_ref[half] = (total[half] + partial(half)).astype(out_ref.dtype)


def product(rows, columns):
    steps, part, tokens = rows.shape[0], *rows.shape[3:]
    n = columns.shape[1]
    in_specs = [
        pl.BlockSpec((1, 2, 2, part, tokens), lambda k: (k, 0, 0, 0, 0)),
        pl.BlockSpec((2, n, tokens), lambda k: (k, 0, 0)),
    ]
    whole = pl.BlockSpec((2, part, n), lambda k: (0, 0, 0))
    return pl.pallas_call(
        functools.partial(product_body, steps=steps),
        grid=(steps,),
        in_specs=in_specs,
        out_specs=whole,
        out_shape=jax.ShapeDtypeStruct((2, part, n), jnp.bfloat16),
        scratch_shapes=[pltpu.VMEM((2, part, n), jnp.float32)],
        compiler_params=pltpu.CompilerParams(
            dimension_semantics=("arbitrary",), vmem_limit_bytes=56 * 1024 * 1024
        ),
        cost_estimate=pl.CostEstimate(
            flops=2 * 2 * part * n * tokens * RING, bytes_accessed=16 * 1024 * 1024, transcendentals=0
        ),
    )(rows, columns)


def along_x(step):
    return [
        ((x * 2 + y) * 2 + c, ((x + step) % 4 * 2 + y) * 2 + c)
        for x in range(4) for y in range(2) for c in range(2)
    ]


ACROSS_Y = [(t, t ^ 2) for t in range(16)]
ACROSS_CORE = [(t, t ^ 1) for t in range(16)]
ARRIVALS = ((0, 0), (3, 0), (1, 0), (0, 1), (3, 1), (2, 0), (1, 1), (2, 1))


def own_body(where_ref, own0, own1, twin0, twin1, columns_ref, out_ref, total):
    k = pl.program_id(0)
    y, c = where_ref[8], where_ref[9]

    def partial(own, twin):
        return sum(
            lax.dot_general(
                rows_ref[0], columns_ref[i], (((1,), (1,)), ((), ())), preferred_element_type=jnp.float32
            )
            for rows_ref, i in ((own, c), (twin, 1 - c))
        )

    for half, (own, twin) in enumerate(((own0, twin0), (own1, twin1))):
        @pl.when(k == 0)
        def _():
            total[half] = partial(own, twin)

        @pl.when((k > 0) & (k < 3))
        def _():
            total[half] += partial(own, twin)

        @pl.when(k == 3)
        def _():
            out_ref[half ^ y] = total[half] + partial(own, twin)


def own_product(own, twin, columns, t):
    part, tokens = own.shape[1:]
    n = columns.shape[1]
    table = [
        [ARRIVALS.index(((k - x) % 4, y)) for y in range(2) for k in range(4)] for x in range(4)
    ]
    row = lax.dynamic_index_in_dim(jnp.array(table, jnp.int32), t // 4, keepdims=False)
    where = jnp.concatenate([row, jnp.stack([(t // 2) % 2, t % 2]).astype(jnp.int32)])
    block = (1, part, tokens)
    first = pl.BlockSpec(block, lambda k, s: (s[k], 0, 0))
    second = pl.BlockSpec(block, lambda k, s: (s[4 + k], 0, 0))
    return pl.pallas_call(
        own_body,
        grid_spec=pltpu.PrefetchScalarGridSpec(
            num_scalar_prefetch=1,
            grid=(4,),
            in_specs=[first, second, first, second, pl.BlockSpec((2, n, tokens), lambda k, s: (k, 0, 0))],
            out_specs=pl.BlockSpec((2, part, n), lambda k, s: (0, 0, 0)),
            scratch_shapes=[pltpu.VMEM((2, part, n), jnp.float32)],
        ),
        out_shape=jax.ShapeDtypeStruct((2, part, n), jnp.float32),
        compiler_params=pltpu.CompilerParams(
            dimension_semantics=("arbitrary",), vmem_limit_bytes=56 * 1024 * 1024
        ),
        cost_estimate=pl.CostEstimate(
            flops=2 * 2 * part * n * tokens * RING, bytes_accessed=16 * 1024 * 1024, transcendentals=0
        ),
    )(where, own, own, twin, twin, columns)


def put(columns, block, offset, start=0):
    return lax.dynamic_update_slice(columns, block[None], (PLACES.index(offset), start, 0))


def shards(out_grad, down_weight, gate_pre):
    n, tokens = down_weight.shape[0], out_grad.shape[0]
    part = n // 2
    hidden_grad = lax.dot_general(
        down_weight, out_grad, (((1,), (1,)), ((), ())), preferred_element_type=jnp.float32
    ).astype(jnp.bfloat16)
    up_grad = (hidden_grad.astype(jnp.float32) * jax.nn.silu(gate_pre.T.astype(jnp.float32))).astype(
        jnp.bfloat16
    )
    h = lax.axis_index("dp") // RING
    t = lax.axis_index("tensor")
    b, half = t // RING, (t // 2) % 2

    low, high = up_grad[:part], up_grad[part:]
    got = [
        lax.ppermute(jnp.where((b ^ turn) == 0, low, high), BOTH, in_plane(turn)) for turn in range(2)
    ]
    up, down = lax.ppermute(up_grad, "dp", along_z(1)), lax.ppermute(up_grad, "dp", along_z(-1))
    got[0], got[1], up, down, up_grad = lax.optimization_barrier((got[0], got[1], up, down, up_grad))

    first_turn = half ^ (1 - h)
    theirs = jnp.where(first_turn == 0, got[0], got[1])
    ours = jnp.where(first_turn == 0, got[1], got[0])
    theirs = lax.ppermute(theirs, BOTH, shifted())
    columns = jnp.broadcast_to(up_grad[None], (RING, n, tokens))
    columns = put(put(columns, up, RING - 1), down, 1)
    theirs, up, down, ours, columns = lax.optimization_barrier((theirs, up, down, ours, columns))
    rows_theirs = lax.all_gather(theirs, "tensor", axis=0).reshape(4, 2, 2, part, tokens)

    up, down = lax.ppermute(up, "dp", along_z(1)), lax.ppermute(down, "dp", along_z(-1))
    ours = lax.ppermute(ours, BOTH, shifted())
    up, down, ours, columns = lax.optimization_barrier((up, down, ours, columns))
    columns = put(put(columns, up, RING - 2), down, 2)
    up, down = lax.ppermute(up, "dp", along_z(1)), lax.ppermute(down, "dp", along_z(-1))
    before, after = lax.ppermute(ours, "tensor", along_x(1)), lax.ppermute(ours, "tensor", along_x(-1))
    beside = lax.ppermute(ours, "tensor", ACROSS_Y)
    up, down, columns, before, after, beside = lax.optimization_barrier(
        (up, down, columns, before, after, beside)
    )

    columns = put(put(columns, up, RING - 3), down, 3)
    up = lax.ppermute(up[:part], "dp", along_z(1))
    down = lax.ppermute(down[part:], "dp", along_z(-1))
    near = jnp.stack([ours, before, after, beside])
    before_beside = lax.ppermute(beside, "tensor", along_x(1))
    far = lax.ppermute(after, "tensor", along_x(-1))
    after_beside = lax.ppermute(after, "tensor", ACROSS_Y)
    near_twin = lax.ppermute(near, "tensor", ACROSS_CORE)
    up, down, columns, before_beside, far, after_beside, near_twin = lax.optimization_barrier(
        (up, down, columns, before_beside, far, after_beside, near_twin)
    )
    columns = put(put(columns, up, RING // 2), down, RING // 2, part)

    cut = part // 32 * 16 + 16
    last = jnp.concatenate(
        [
            lax.ppermute(before_beside[:cut], "tensor", along_x(1)),
            lax.ppermute(after_beside[cut:], "tensor", along_x(-1)),
        ],
        axis=0,
    )
    middle = jnp.stack([before_beside, far, after_beside])
    middle_twin = lax.ppermute(middle, "tensor", ACROSS_CORE)
    last_twin = lax.ppermute(last, "tensor", ACROSS_CORE)
    own = jnp.concatenate([near, middle, last[None]])
    twin = jnp.concatenate([near_twin, middle_twin, last_twin[None]])

    sent = lax.ppermute(product(rows_theirs, columns), "dp", ACROSS)
    kept = own_product(own, twin, columns, t)
    total = tokens * lax.axis_size("dp")
    return ((kept + sent.astype(jnp.float32)) * (1.0 / total)).reshape(n, n)


def solution(mesh):
    placed = (P("dp", None), P("tensor", None), P("dp", "tensor"))
    return jax.shard_map(
        shards, mesh=mesh, in_specs=placed, out_specs=P("dp", "tensor"), check_vma=False
    )
```

```python
import jax
import jax.numpy as jnp
from jax import lax
from jax.sharding import PartitionSpec as P

BOTH = ("dp", "tensor")
RING = 8
PLACES = (0, 4, 1, 7, 2, 6, 3, 5)


def place(offset, half):
    k = PLACES.index(offset)
    return (k // 2) * 4 + half * 2 + k % 2


def in_plane(turn):
    pairs = []
    for h in range(2):
        for source in range(RING):
            for b in range(2):
                for z in range(RING):
                    plane = (h * RING + source) * 16
                    pairs.append((plane + b * RING + z, plane + place((source - z) % RING, b ^ turn)))
    return pairs


def shifted():
    pairs = []
    for h in range(2):
        for z in range(RING):
            for offset in range(RING):
                for half in range(2):
                    t = place(offset, half)
                    pairs.append(((h * RING + (z + offset) % RING) * 16 + t, (h * RING + z) * 16 + t))
    return pairs


def along_z(step):
    return [(h * RING + z, h * RING + (z + step) % RING) for h in range(2) for z in range(RING)]


ACROSS = [(i, (i + RING) % 16) for i in range(16)]


def along_x(step):
    return [
        ((x * 2 + y) * 2 + c, ((x + step) % 4 * 2 + y) * 2 + c)
        for x in range(4) for y in range(2) for c in range(2)
    ]


ACROSS_Y = [(t, t ^ 2) for t in range(16)]
ACROSS_CORE = [(t, t ^ 1) for t in range(16)]
def put(columns, block, offset, t, start=0):
    k, core = divmod(PLACES.index(offset), 2)
    return lax.dynamic_update_slice(
        columns, block[None, None], (core ^ (t % 2), (k - t // 4) % 4, start, 0)
    )


def first_half(piece):
    before, after = lax.ppermute(piece, "tensor", along_x(1)), lax.ppermute(piece, "tensor", along_x(-1))
    beside = lax.ppermute(piece, "tensor", ACROSS_Y)
    before_beside = lax.ppermute(beside, "tensor", along_x(1))
    far = lax.ppermute(after, "tensor", along_x(-1))
    after_beside = lax.ppermute(after, "tensor", ACROSS_Y)
    return piece, before, after, beside, before_beside, far, after_beside


def gathered(pieces, t):
    piece, before, after, beside, before_beside, far, after_beside = pieces
    part = piece.shape[0]
    y = (t // 2) % 2

    def placed(rows, block, x, beside, start=0):
        return lax.dynamic_update_slice(rows, block[None, None], (x, beside ^ y, start, 0))

    cut = part // 32 * 16 + 16
    far_low = lax.ppermute(before_beside[:cut], "tensor", along_x(1))
    far_high = lax.ppermute(after_beside[cut:], "tensor", along_x(-1))

    own = jnp.broadcast_to(piece[None, None], (4, 2) + piece.shape)
    own = placed(placed(placed(own, before, 3, 0), after, 1, 0), beside, 0, 1)
    own = placed(placed(placed(own, before_beside, 3, 1), far, 2, 0), after_beside, 1, 1)
    own = placed(placed(own, far_low, 2, 1), far_high, 2, 1, cut)
    own = own.reshape(4, 2 * part, piece.shape[1])
    return own, lax.ppermute(own, "tensor", ACROSS_CORE)


def product(rows, columns):
    return sum(
        lax.dot_general(
            rows[i], columns[i], (((0, 2), (0, 2)), ((), ())), preferred_element_type=jnp.float32
        )
        for i in range(2)
    )


def shards(out_grad, down_weight, gate_pre):
    n, tokens = down_weight.shape[0], out_grad.shape[0]
    part = n // 2
    hidden_grad = lax.dot_general(
        down_weight, out_grad, (((1,), (1,)), ((), ())), preferred_element_type=jnp.float32
    ).astype(jnp.bfloat16)
    up_grad = (hidden_grad.astype(jnp.float32) * jax.nn.silu(gate_pre.T.astype(jnp.float32))).astype(
        jnp.bfloat16
    )
    h = lax.axis_index("dp") // RING
    t = lax.axis_index("tensor")
    b, half = t // RING, (t // 2) % 2

    low, high = up_grad[:part], up_grad[part:]
    got = [
        lax.ppermute(jnp.where((b ^ turn) == 0, low, high), BOTH, in_plane(turn)) for turn in range(2)
    ]
    up, down = lax.ppermute(up_grad, "dp", along_z(1)), lax.ppermute(up_grad, "dp", along_z(-1))
    got[0], got[1], up, down, up_grad = lax.optimization_barrier((got[0], got[1], up, down, up_grad))

    first_turn = half ^ (1 - h)
    theirs = jnp.where(first_turn == 0, got[0], got[1])
    ours = jnp.where(first_turn == 0, got[1], got[0])
    theirs = lax.ppermute(theirs, BOTH, shifted())
    columns = jnp.broadcast_to(up_grad, (2, 4, n, tokens))
    columns = put(put(columns, up, RING - 1, t), down, 1, t)
    theirs, up, down, ours, columns = lax.optimization_barrier((theirs, up, down, ours, columns))

    pieces = first_half(theirs)
    up, down = lax.ppermute(up, "dp", along_z(1)), lax.ppermute(down, "dp", along_z(-1))
    columns = put(put(columns, up, RING - 2, t), down, 2, t)
    up, down, ours = lax.optimization_barrier((up, down, ours))

    ours = lax.ppermute(ours, BOTH, shifted())
    rows_theirs = gathered(pieces, t)
    up, down = lax.ppermute(up, "dp", along_z(1)), lax.ppermute(down, "dp", along_z(-1))
    columns = put(put(columns, up, RING - 3, t), down, 3, t)
    pieces = first_half(ours)
    up = lax.ppermute(up[:part], "dp", along_z(1))
    down = lax.ppermute(down[part:], "dp", along_z(-1))
    columns = put(put(columns, up, RING // 2, t), down, RING // 2, t, part)

    partial = product(rows_theirs, columns).astype(jnp.bfloat16)
    sent = lax.ppermute(partial, "dp", ACROSS)
    _, pieces = lax.optimization_barrier((partial, pieces))
    kept = product(gathered(pieces, t), columns)
    total = tokens * lax.axis_size("dp")
    return (kept + sent.astype(jnp.float32)) * (1.0 / total)


def solution(mesh):
    placed = (P("dp", None), P("tensor", None), P("dp", "tensor"))
    return jax.shard_map(
        shards, mesh=mesh, in_specs=placed, out_specs=P("dp", "tensor"), check_vma=False
    )
```

```python
import jax
import jax.numpy as jnp
from jax import lax
from jax.sharding import PartitionSpec as P

BOTH = ("dp", "tensor")
RING = 8
PLACES = (0, 4, 1, 7, 2, 6, 3, 5)


def place(offset, half):
    k = PLACES.index(offset)
    return (k // 2) * 4 + half * 2 + k % 2


def in_plane(turn):
    pairs = []
    for h in range(2):
        for source in range(RING):
            for b in range(2):
                for z in range(RING):
                    plane = (h * RING + source) * 16
                    pairs.append((plane + b * RING + z, plane + place((source - z) % RING, b ^ turn)))
    return pairs


def shifted():
    pairs = []
    for h in range(2):
        for z in range(RING):
            for offset in range(RING):
                for half in range(2):
                    t = place(offset, half)
                    pairs.append(((h * RING + (z + offset) % RING) * 16 + t, (h * RING + z) * 16 + t))
    return pairs


def along_z(step):
    return [(h * RING + z, h * RING + (z + step) % RING) for h in range(2) for z in range(RING)]


ACROSS = [(i, (i + RING) % 16) for i in range(16)]


def along_x(step):
    return [
        ((x * 2 + y) * 2 + c, ((x + step) % 4 * 2 + y) * 2 + c)
        for x in range(4) for y in range(2) for c in range(2)
    ]


ACROSS_Y = [(t, t ^ 2) for t in range(16)]
ACROSS_CORE = [(t, t ^ 1) for t in range(16)]
def neighbours(piece):
    return [
        lax.ppermute(piece, "tensor", pairs) for pairs in (along_x(1), along_x(-1), ACROSS_Y)
    ]


def second(before, after, beside):
    return [
        lax.ppermute(beside, "tensor", along_x(1)),
        lax.ppermute(after, "tensor", along_x(-1)),
        lax.ppermute(after, "tensor", ACROSS_Y),
    ]


def last(before_beside, far, after_beside):
    cut = far.shape[0] // 32 * 16 + 16
    return [
        lax.ppermute(before_beside[:cut], "tensor", along_x(1)),
        lax.ppermute(after_beside[cut:], "tensor", along_x(-1)),
    ]


def assembled(piece, near, middle, ends, t):
    part = piece.shape[0]
    x, y = t // 4, (t // 2) % 2
    own = jnp.broadcast_to(piece[None, None], (4, 2) + piece.shape)
    placed = zip((*near, *middle, *ends), (3, 1, 0, 3, 2, 1, 2, 2), (0, 0, 1, 1, 0, 1, 1, 1))
    for block, ahead, beside in placed:
        start = part - block.shape[0] if block is ends[1] else 0
        own = lax.dynamic_update_slice(
            own, block[None, None], ((x + ahead) % 4, beside ^ y, start, 0)
        )
    return own.reshape(4, 2 * part, piece.shape[1])


def product(rows, columns):
    return lax.dot_general(
        rows, columns, (((0, 2), (0, 2)), ((), ())), preferred_element_type=jnp.float32
    )


def shards(out_grad, down_weight, gate_pre):
    n, tokens = down_weight.shape[0], out_grad.shape[0]
    part = n // 2
    hidden_grad = lax.dot_general(
        down_weight, out_grad, (((1,), (1,)), ((), ())), preferred_element_type=jnp.float32
    ).astype(jnp.bfloat16)
    up_grad = (hidden_grad.astype(jnp.float32) * jax.nn.silu(gate_pre.T.astype(jnp.float32))).astype(
        jnp.bfloat16
    )
    h = lax.axis_index("dp") // RING
    t = lax.axis_index("tensor")
    b, half = t // RING, (t // 2) % 2

    low, high = up_grad[:part], up_grad[part:]
    got = [
        lax.ppermute(jnp.where((b ^ turn) == 0, low, high), BOTH, in_plane(turn)) for turn in range(2)
    ]
    up, down = lax.ppermute(up_grad, "dp", along_z(1)), lax.ppermute(up_grad, "dp", along_z(-1))
    got[0], got[1], up, down, up_grad = lax.optimization_barrier((got[0], got[1], up, down, up_grad))

    first_turn = half ^ (1 - h)
    theirs = jnp.where(first_turn == 0, got[0], got[1])
    ours = jnp.where(first_turn == 0, got[1], got[0])
    theirs = lax.ppermute(theirs, BOTH, shifted())
    early = jnp.broadcast_to(up_grad, (5, n, tokens))
    early = early.at[1].set(down).at[2].set(up)
    theirs, up, down, ours, early = lax.optimization_barrier((theirs, up, down, ours, early))

    near = neighbours(theirs)
    ours = lax.ppermute(ours, BOTH, shifted())
    near, ours, up, down = lax.optimization_barrier((near, ours, up, down))
    rows_ours = lax.all_gather(ours, "tensor", axis=0).reshape(4, 2, 2, part, tokens)

    middle = second(*near)
    up, down = lax.ppermute(up, "dp", along_z(1)), lax.ppermute(down, "dp", along_z(-1))
    early = early.at[3].set(down).at[4].set(up)
    middle, _ = lax.optimization_barrier((middle, (up, down)))

    ends = last(*middle)
    up, down = lax.ppermute(up, "dp", along_z(1)), lax.ppermute(down, "dp", along_z(-1))
    own = assembled(theirs, near, middle, ends, t)
    own, _ = lax.optimization_barrier((own, (up, down)))

    twin = lax.ppermute(own, "tensor", ACROSS_CORE)
    opposite = [
        lax.ppermute(up[:part], "dp", along_z(1)), lax.ppermute(down[part:], "dp", along_z(-1))
    ]

    twin, rows_ours = lax.optimization_barrier((twin, rows_ours))

    def their_rows(offset):
        k, core = divmod(PLACES.index(offset), 2)
        return jnp.where(t % 2 == core, own[k], twin[k])

    def our_rows(offset):
        k, core = divmod(PLACES.index(offset), 2)
        return rows_ours[k, :, core].reshape(n, tokens)

    def stacked(rows, offsets):
        return jnp.stack([rows(offset) for offset in offsets])

    partial = product(stacked(their_rows, (0, 1, 7, 2, 6)), early)
    their_late = stacked(their_rows, (3, 5, 4))
    partial, their_late, opposite = lax.optimization_barrier((partial, their_late, opposite))
    late = jnp.stack([down, up, jnp.concatenate(opposite)])
    partial += product(their_late, late)
    sent = lax.ppermute(partial.astype(jnp.bfloat16), "dp", ACROSS)
    kept = product(stacked(our_rows, (0, 1, 7, 2, 6)), early) + product(stacked(our_rows, (3, 5, 4)), late)
    total = tokens * lax.axis_size("dp")
    return (kept + sent.astype(jnp.float32)) * (1.0 / total)


def solution(mesh):
    placed = (P("dp", None), P("tensor", None), P("dp", "tensor"))
    return jax.shard_map(
        shards, mesh=mesh, in_specs=placed, out_specs=P("dp", "tensor"), check_vma=False
    )
```

```python
import jax
import jax.numpy as jnp
from jax import lax
from jax.sharding import PartitionSpec as P

BOTH = ("dp", "tensor")
RING = 8
PLACES = (0, 4, 1, 7, 2, 6, 3, 5)


def place(offset, other):
    k = PLACES.index(offset)
    return (k // 2) * 4 + other * 2 + k % 2


def in_plane():
    pairs = []
    for h in range(2):
        for source in range(RING):
            for b in range(2):
                for z in range(RING):
                    plane = (h * RING + source) * 16
                    pairs.append((plane + b * RING + z, plane + place((source - z) % RING, b ^ h)))
    return pairs


def shifted():
    pairs = []
    for h in range(2):
        for z in range(RING):
            for offset in range(RING):
                for other in range(2):
                    t = place(offset, other)
                    pairs.append(((h * RING + (z + offset) % RING) * 16 + t, (h * RING + z) * 16 + t))
    return pairs


def along_z(step):
    return [(h * RING + z, h * RING + (z + step) % RING) for h in range(2) for z in range(RING)]


ACROSS = [(i, (i + RING) % 16) for i in range(16)]


def product(rows, columns):
    return lax.dot_general(
        rows, columns, (((0, 2), (0, 2)), ((), ())), preferred_element_type=jnp.float32
    )


def put(columns, block, offset, start=0):
    return lax.dynamic_update_slice(columns, block[None], (PLACES.index(offset), start, 0))


def shards(out_grad, down_weight, gate_pre):
    n, tokens = down_weight.shape[0], out_grad.shape[0]
    cut = n // 32 * 16 + 16
    hidden_grad = lax.dot_general(
        down_weight, out_grad, (((1,), (1,)), ((), ())), preferred_element_type=jnp.float32
    ).astype(jnp.bfloat16)
    up_grad = (hidden_grad.astype(jnp.float32) * jax.nn.silu(gate_pre.T.astype(jnp.float32))).astype(
        jnp.bfloat16
    )
    rows = lax.ppermute(up_grad, BOTH, in_plane())
    up, down = lax.ppermute(up_grad, "dp", along_z(1)), lax.ppermute(up_grad, "dp", along_z(-1))
    rows, up, down, up_grad = lax.optimization_barrier((rows, up, down, up_grad))

    rows = lax.ppermute(rows, BOTH, shifted())
    columns = jnp.broadcast_to(up_grad[None], (RING, n, tokens))
    columns = put(put(columns, up, RING - 1), down, 1)
    rows, up, down, columns = lax.optimization_barrier((rows, up, down, columns))
    rows = lax.all_gather(rows, "tensor", axis=0).reshape(4, 2, 2, n, tokens)

    for step in range(2, RING // 2):
        up, down = lax.ppermute(up, "dp", along_z(1)), lax.ppermute(down, "dp", along_z(-1))
        columns = put(put(columns, up, RING - step), down, step)
    up = lax.ppermute(up[:cut], "dp", along_z(1))
    down = lax.ppermute(down[cut:], "dp", along_z(-1))
    columns = put(put(columns, up, RING // 2), down, RING // 2, cut)

    def partial(rows, other):
        return product(rows[:, other].reshape(RING, n, tokens), columns)

    theirs = partial(rows, 1).astype(jnp.bfloat16)
    sent = lax.ppermute(theirs, "dp", ACROSS)
    rows, _ = lax.optimization_barrier((rows, theirs))
    kept = lax.optimization_barrier(partial(rows, 0))
    total = tokens * lax.axis_size("dp")
    return (kept + sent.astype(jnp.float32)) * (1.0 / total)


def solution(mesh):
    placed = (P("dp", None), P("tensor", None), P("dp", "tensor"))
    return jax.shard_map(
        shards, mesh=mesh, in_specs=placed, out_specs=P("dp", "tensor"), check_vma=False
    )
```

```python
import jax
import jax.numpy as jnp
from jax import lax
from jax.sharding import PartitionSpec as P

BOTH = ("dp", "tensor")
RING = 8
PLACES = (0, 4, 1, 7, 2, 6, 3, 5)


def place(offset, other):
    k = PLACES.index(offset)
    return (k // 2) * 4 + other * 2 + k % 2


def in_plane():
    pairs = []
    for h in range(2):
        for source in range(RING):
            for b in range(2):
                for z in range(RING):
                    plane = (h * RING + source) * 16
                    pairs.append((plane + b * RING + z, plane + place((source - z) % RING, b ^ h)))
    return pairs


def shifted():
    pairs = []
    for h in range(2):
        for z in range(RING):
            for offset in range(RING):
                for other in range(2):
                    t = place(offset, other)
                    pairs.append(((h * RING + (z + offset) % RING) * 16 + t, (h * RING + z) * 16 + t))
    return pairs


def along_z(step):
    return [(h * RING + z, h * RING + (z + step) % RING) for h in range(2) for z in range(RING)]


ACROSS = [(i, (i + RING) % 16) for i in range(16)]


def put(columns, block, offset, start=0):
    tokens = block.shape[1]
    return lax.dynamic_update_slice(columns, block, (start, PLACES.index(offset) * tokens))


def shards(out_grad, down_weight, gate_pre):
    n, tokens = down_weight.shape[0], out_grad.shape[0]
    cut = n // 32 * 16 + 16
    hidden_grad = lax.dot_general(
        down_weight, out_grad, (((1,), (1,)), ((), ())), preferred_element_type=jnp.float32
    ).astype(jnp.bfloat16)
    up_grad = (hidden_grad.astype(jnp.float32) * jax.nn.silu(gate_pre.T.astype(jnp.float32))).astype(
        jnp.bfloat16
    )
    rows = lax.ppermute(lax.ppermute(up_grad, BOTH, in_plane()), BOTH, shifted())
    rows, up_grad = lax.optimization_barrier((rows, up_grad))
    rows = lax.all_gather(rows, "tensor", axis=0).reshape(4, 2, 2, n, tokens)

    columns = put(jnp.zeros((n, RING * tokens), jnp.bfloat16), up_grad, 0)
    up, down = up_grad, up_grad
    for step in range(1, RING // 2):
        up, down = lax.ppermute(up, "dp", along_z(1)), lax.ppermute(down, "dp", along_z(-1))
        columns = put(put(columns, up, RING - step), down, step)
    up = lax.ppermute(up[:cut], "dp", along_z(1))
    down = lax.ppermute(down[cut:], "dp", along_z(-1))
    columns = put(put(columns, up, RING // 2), down, RING // 2, cut)

    def partial(rows, other):
        blocks = [rows[k // 2, other, k % 2] for k in range(RING)]
        return lax.dot_general(
            jnp.concatenate(blocks, axis=1), columns, (((1,), (1,)), ((), ())),
            preferred_element_type=jnp.float32,
        )

    theirs = partial(rows, 1).astype(jnp.bfloat16)
    sent = lax.ppermute(theirs, "dp", ACROSS)
    rows, _ = lax.optimization_barrier((rows, theirs))
    kept = lax.optimization_barrier(partial(rows, 0))
    total = tokens * lax.axis_size("dp")
    return (kept + sent.astype(jnp.float32)) * (1.0 / total)


def solution(mesh):
    placed = (P("dp", None), P("tensor", None), P("dp", "tensor"))
    return jax.shard_map(
        shards, mesh=mesh, in_specs=placed, out_specs=P("dp", "tensor"), check_vma=False
    )
```

```python
import functools

import jax
import jax.numpy as jnp
from jax import lax
from jax.experimental import pallas as pl
from jax.experimental.pallas import tpu as pltpu
from jax.sharding import PartitionSpec as P

BOTH = ("dp", "tensor")
RING = 8
PLACES = ((0, 4, 1, 7, 2, 6, 3, 5), (1, 7, 0, 4, 3, 5, 2, 6))


def place(offset, other, second):
    k = PLACES[second].index(offset)
    return (k // 2) * 4 + other * 2 + k % 2


def in_plane(second):
    pairs = []
    for h in range(2):
        for source in range(RING):
            for b in range(2):
                for z in range(RING):
                    plane = (h * RING + source) * 16
                    pairs.append((plane + b * RING + z, plane + place((source - z) % RING, b ^ h, second)))
    return pairs


def shifted(second):
    pairs = []
    for h in range(2):
        for z in range(RING):
            for offset in range(RING):
                for other in range(2):
                    t = place(offset, other, second)
                    pairs.append(((h * RING + (z + offset) % RING) * 16 + t, (h * RING + z) * 16 + t))
    return pairs


def along_z(step):
    return [(h * RING + z, h * RING + (z + step) % RING) for h in range(2) for z in range(RING)]


ACROSS = [(i, (i + RING) % 16) for i in range(16)]


def product_body(first_ref, second_ref, columns_ref, out_ref, total, *, cut):
    k = pl.program_id(0)

    def partial(ref, low, high):
        return sum(
            lax.dot_general(
                ref[0, 0, core, low:high], columns_ref[core], (((1,), (1,)), ((), ())),
                preferred_element_type=jnp.float32,
            )
            for core in range(2)
        )

    n = out_ref.shape[0]
    for ref, low, high in ((first_ref, 0, cut), (second_ref, cut, n)):
        @pl.when(k == 0)
        def _():
            total[low:high] = partial(ref, low, high)

        @pl.when((k > 0) & (k < 3))
        def _():
            total[low:high] += partial(ref, low, high)

        @pl.when(k == 3)
        def _():
            out_ref[low:high] = (total[low:high] + partial(ref, low, high)).astype(out_ref.dtype)


def product(rows, columns, other, cut, kind):
    n, tokens = columns.shape[1:]
    block = (1, 1, 2, n, tokens)
    return pl.pallas_call(
        functools.partial(product_body, cut=cut),
        grid=(4,),
        in_specs=[
            pl.BlockSpec(block, lambda k: (k, other, 0, 0, 0)),
            pl.BlockSpec(block, lambda k: (k ^ 1, other, 0, 0, 0)),
            pl.BlockSpec((2, n, tokens), lambda k: (k, 0, 0)),
        ],
        out_specs=pl.BlockSpec((n, n), lambda k: (0, 0)),
        out_shape=jax.ShapeDtypeStruct((n, n), kind),
        scratch_shapes=[pltpu.VMEM((n, n), jnp.float32)],
        compiler_params=pltpu.CompilerParams(
            dimension_semantics=("arbitrary",), vmem_limit_bytes=56 * 1024 * 1024
        ),
        cost_estimate=pl.CostEstimate(
            flops=2 * n * n * tokens * RING, bytes_accessed=24 * 1024 * 1024, transcendentals=0
        ),
    )(rows, rows, columns)


def put(columns, block, offset, start=0):
    return lax.dynamic_update_slice(columns, block[None], (PLACES[0].index(offset), start, 0))


def shards(out_grad, down_weight, gate_pre):
    n, tokens = down_weight.shape[0], out_grad.shape[0]
    cut = n // 32 * 16 + 16
    hidden_grad = lax.dot_general(
        down_weight, out_grad, (((1,), (1,)), ((), ())), preferred_element_type=jnp.float32
    ).astype(jnp.bfloat16)
    up_grad = (hidden_grad.astype(jnp.float32) * jax.nn.silu(gate_pre.T.astype(jnp.float32))).astype(
        jnp.bfloat16
    )
    parts = [
        lax.ppermute(lax.ppermute(piece, BOTH, in_plane(second)), BOTH, shifted(second))
        for second, piece in enumerate((up_grad[:cut], up_grad[cut:]))
    ]
    rows, up_grad = lax.optimization_barrier((jnp.concatenate(parts), up_grad))
    rows = lax.all_gather(rows, "tensor", axis=0).reshape(4, 2, 2, n, tokens)

    columns = jnp.broadcast_to(up_grad[None], (RING, n, tokens))
    up, down = up_grad, up_grad
    for step in range(1, RING // 2):
        up, down = lax.ppermute(up, "dp", along_z(1)), lax.ppermute(down, "dp", along_z(-1))
        columns = put(put(columns, up, RING - step), down, step)
    up = lax.ppermute(up[:cut], "dp", along_z(1))
    down = lax.ppermute(down[cut:], "dp", along_z(-1))
    columns = put(put(columns, up, RING // 2), down, RING // 2, cut)

    sent = lax.ppermute(product(rows, columns, 1, cut, jnp.bfloat16), "dp", ACROSS)
    kept = product(rows, columns, 0, cut, jnp.float32)
    total = tokens * lax.axis_size("dp")
    return (kept + sent.astype(jnp.float32)) * (1.0 / total)


def solution(mesh):
    placed = (P("dp", None), P("tensor", None), P("dp", "tensor"))
    return jax.shard_map(
        shards, mesh=mesh, in_specs=placed, out_specs=P("dp", "tensor"), check_vma=False
    )
```

```python
import jax
import jax.numpy as jnp
from jax import lax
from jax.experimental import pallas as pl
from jax.experimental.pallas import tpu as pltpu
from jax.sharding import PartitionSpec as P

BOTH = ("dp", "tensor")
RING = 8
PLACES = ((0, 4, 1, 7, 2, 6, 3, 5), (1, 7, 0, 4, 3, 5, 2, 6))


def place(offset, other, second):
    k = PLACES[second].index(offset)
    return (k // 2) * 4 + other * 2 + k % 2


def in_plane(second):
    pairs = []
    for h in range(2):
        for source in range(RING):
            for b in range(2):
                for z in range(RING):
                    plane = (h * RING + source) * 16
                    pairs.append((plane + b * RING + z, plane + place((source - z) % RING, b ^ h, second)))
    return pairs


def shifted(second):
    pairs = []
    for h in range(2):
        for z in range(RING):
            for offset in range(RING):
                for other in range(2):
                    t = place(offset, other, second)
                    pairs.append(((h * RING + (z + offset) % RING) * 16 + t, (h * RING + z) * 16 + t))
    return pairs


def along_z(step):
    return [(h * RING + z, h * RING + (z + step) % RING) for h in range(2) for z in range(RING)]


ACROSS = [(i, (i + RING) % 16) for i in range(16)]


def product_body(rows_ref, columns_ref, out_ref, total):
    k = pl.program_id(0)
    count = out_ref.shape[0]

    def partial():
        return sum(
            lax.dot_general(
                rows_ref[0, 0, core, :count], columns_ref[2 * k + core], (((1,), (1,)), ((), ())),
                preferred_element_type=jnp.float32,
            )
            for core in range(2)
        )

    @pl.when(k == 0)
    def _():
        total[...] = partial()

    @pl.when((k > 0) & (k < 3))
    def _():
        total[...] += partial()

    @pl.when(k == 3)
    def _():
        out_ref[...] = (total[...] + partial()).astype(out_ref.dtype)


def product(rows, columns, other, second, cut, kind):
    n, tokens = columns.shape[1:]
    count = n - cut if second else cut
    return pl.pallas_call(
        product_body,
        grid=(4,),
        in_specs=[
            pl.BlockSpec((1, 1, 2, cut, tokens), lambda k: (k ^ second, other, 0, second, 0)),
            pl.BlockSpec(memory_space=pltpu.VMEM),
        ],
        out_specs=pl.BlockSpec((count, n), lambda k: (0, 0)),
        out_shape=jax.ShapeDtypeStruct((count, n), kind),
        scratch_shapes=[pltpu.VMEM((count, n), jnp.float32)],
        compiler_params=pltpu.CompilerParams(
            dimension_semantics=("arbitrary",), vmem_limit_bytes=48 * 1024 * 1024
        ),
        cost_estimate=pl.CostEstimate(
            flops=2 * count * n * tokens * RING, bytes_accessed=8 * 1024 * 1024, transcendentals=0
        ),
    )(rows, columns)


def put(columns, block, offset, start=0):
    return lax.dynamic_update_slice(columns, block[None], (PLACES[0].index(offset), start, 0))


def shards(out_grad, down_weight, gate_pre):
    n, tokens = down_weight.shape[0], out_grad.shape[0]
    cut = n // 32 * 16 + 16
    hidden_grad = lax.dot_general(
        down_weight, out_grad, (((1,), (1,)), ((), ())), preferred_element_type=jnp.float32
    ).astype(jnp.bfloat16)
    up_grad = (hidden_grad.astype(jnp.float32) * jax.nn.silu(gate_pre.T.astype(jnp.float32))).astype(
        jnp.bfloat16
    )
    parts = [
        lax.ppermute(lax.ppermute(piece, BOTH, in_plane(second)), BOTH, shifted(second))
        for second, piece in enumerate((up_grad[:cut], up_grad[cut:]))
    ]
    rows, up_grad = lax.optimization_barrier((jnp.concatenate(parts), up_grad))
    rows = lax.all_gather(rows, "tensor", axis=0).reshape(4, 2, 2, n, tokens)

    columns = jnp.broadcast_to(up_grad[None], (RING, n, tokens))
    up, down = up_grad, up_grad
    for step in range(1, RING // 2):
        up, down = lax.ppermute(up, "dp", along_z(1)), lax.ppermute(down, "dp", along_z(-1))
        columns = put(put(columns, up, RING - step), down, step)
    up = lax.ppermute(up[:cut], "dp", along_z(1))
    down = lax.ppermute(down[cut:], "dp", along_z(-1))
    columns = put(put(columns, up, RING // 2), down, RING // 2, cut)

    total = tokens * lax.axis_size("dp")
    theirs = [
        product(rows, columns, 1, second, cut, jnp.bfloat16).reshape(-1, 16, n) for second in range(2)
    ]
    sent = [lax.ppermute(part, "dp", ACROSS) for part in theirs]
    out = jnp.zeros((n, n), jnp.float32)
    for second in (1, 0):
        ours = product(rows, columns, 0, second, cut, jnp.float32)
        part = (ours + sent[second].reshape(-1, n).astype(jnp.float32)) * (1.0 / total)
        out = lax.dynamic_update_slice(lax.optimization_barrier(out), part, (second * cut, 0))
    return out


def solution(mesh):
    placed = (P("dp", None), P("tensor", None), P("dp", "tensor"))
    return jax.shard_map(
        shards, mesh=mesh, in_specs=placed, out_specs=P("dp", "tensor"), check_vma=False
    )
```

```python
import jax
import jax.numpy as jnp
from jax import lax
from jax.experimental import pallas as pl
from jax.experimental.pallas import tpu as pltpu
from jax.sharding import PartitionSpec as P

BOTH = ("dp", "tensor")
RING = 8
PARTS = 4
PLACES = (0, 4, 1, 7, 2, 6, 3, 5)


def place(offset, other, part):
    pair, core = divmod(PLACES.index(offset), 2)
    return (pair + part) % 4 * 4 + other * 2 + core


def in_plane(part):
    pairs = []
    for h in range(2):
        for source in range(RING):
            for b in range(2):
                for z in range(RING):
                    plane = (h * RING + source) * 16
                    pairs.append((plane + b * RING + z, plane + place((source - z) % RING, b ^ h, part)))
    return pairs


def shifted(part):
    pairs = []
    for h in range(2):
        for z in range(RING):
            for offset in range(RING):
                for other in range(2):
                    t = place(offset, other, part)
                    pairs.append(((h * RING + (z + offset) % RING) * 16 + t, (h * RING + z) * 16 + t))
    return pairs


def along_z(step):
    return [(h * RING + z, h * RING + (z + step) % RING) for h in range(2) for z in range(RING)]


ACROSS = [(i, (i + RING) % 16) for i in range(16)]


def product_body(low_ref, high_ref, columns_ref, out_ref, total):
    k = pl.program_id(0)
    low = low_ref.shape[3]
    high = out_ref.shape[0] - low

    def partial():
        return sum(
            lax.dot_general(
                jnp.concatenate([low_ref[0, 0, core], high_ref[0, 0, core, :high]]),
                columns_ref[2 * k + core], (((1,), (1,)), ((), ())),
                preferred_element_type=jnp.float32,
            )
            for core in range(2)
        )

    @pl.when(k == 0)
    def _():
        total[...] = partial()

    @pl.when((k > 0) & (k < 3))
    def _():
        total[...] += partial()

    @pl.when(k == 3)
    def _():
        out_ref[...] = (total[...] + partial()).astype(out_ref.dtype)


def product(rows, columns, other, second, size, kind):
    n, tokens = columns.shape[1:]
    count = n - 2 * size if second else 2 * size

    def part_spec(part):
        return pl.BlockSpec((1, 1, 2, size, tokens), lambda k: ((k + part) & 3, other, 0, part, 0))

    return pl.pallas_call(
        product_body,
        grid=(4,),
        in_specs=[
            part_spec(2 * second), part_spec(2 * second + 1), pl.BlockSpec(memory_space=pltpu.VMEM)
        ],
        out_specs=pl.BlockSpec((count, n), lambda k: (0, 0)),
        out_shape=jax.ShapeDtypeStruct((count, n), kind),
        scratch_shapes=[pltpu.VMEM((count, n), jnp.float32)],
        compiler_params=pltpu.CompilerParams(
            dimension_semantics=("arbitrary",), vmem_limit_bytes=48 * 1024 * 1024
        ),
        cost_estimate=pl.CostEstimate(
            flops=2 * count * n * tokens * RING, bytes_accessed=8 * 1024 * 1024, transcendentals=0
        ),
    )(rows, rows, columns)


def put(columns, block, offset, start=0):
    return lax.dynamic_update_slice(columns, block[None], (PLACES.index(offset), start, 0))


def shards(out_grad, down_weight, gate_pre):
    n, tokens = down_weight.shape[0], out_grad.shape[0]
    size = -(-n // (16 * PARTS)) * 16
    cut = 2 * size
    hidden_grad = lax.dot_general(
        down_weight, out_grad, (((1,), (1,)), ((), ())), preferred_element_type=jnp.float32
    ).astype(jnp.bfloat16)
    up_grad = (hidden_grad.astype(jnp.float32) * jax.nn.silu(gate_pre.T.astype(jnp.float32))).astype(
        jnp.bfloat16
    )
    parts = [
        lax.ppermute(
            lax.ppermute(up_grad[part * size : (part + 1) * size], BOTH, in_plane(part)), BOTH, shifted(part)
        )
        for part in range(PARTS)
    ]
    rows, up_grad = lax.optimization_barrier((jnp.concatenate(parts), up_grad))
    rows = lax.all_gather(rows, "tensor", axis=0).reshape(4, 2, 2, n, tokens)

    columns = jnp.broadcast_to(up_grad[None], (RING, n, tokens))
    up, down = up_grad, up_grad
    for step in range(1, RING // 2):
        up, down = lax.ppermute(up, "dp", along_z(1)), lax.ppermute(down, "dp", along_z(-1))
        columns = put(put(columns, up, RING - step), down, step)
    up = lax.ppermute(up[:cut], "dp", along_z(1))
    down = lax.ppermute(down[cut:], "dp", along_z(-1))
    columns = put(put(columns, up, RING // 2), down, RING // 2, cut)

    total = tokens * lax.axis_size("dp")
    theirs = [
        product(rows, columns, 1, second, size, jnp.bfloat16).reshape(-1, 16, n) for second in range(2)
    ]
    sent = [lax.ppermute(part, "dp", ACROSS) for part in theirs]
    out = jnp.zeros((n, n), jnp.float32)
    for second in (1, 0):
        ours = product(rows, columns, 0, second, size, jnp.float32)
        part = (ours + sent[second].reshape(-1, n).astype(jnp.float32)) * (1.0 / total)
        out = lax.dynamic_update_slice(lax.optimization_barrier(out), part, (second * cut, 0))
    return out


def solution(mesh):
    placed = (P("dp", None), P("tensor", None), P("dp", "tensor"))
    return jax.shard_map(
        shards, mesh=mesh, in_specs=placed, out_specs=P("dp", "tensor"), check_vma=False
    )
```

```python
import jax
import jax.numpy as jnp
from jax import lax
from jax.experimental import pallas as pl
from jax.experimental.pallas import tpu as pltpu
from jax.sharding import PartitionSpec as P

BOTH = ("dp", "tensor")
RING = 8
PARTS = 4
PLACES = (0, 4, 1, 7, 2, 6, 3, 5)


def place(offset, other, part):
    pair, core = divmod(PLACES.index(offset), 2)
    return (pair + part) % 4 * 4 + other * 2 + core


def in_plane(part):
    pairs = []
    for h in range(2):
        for source in range(RING):
            for b in range(2):
                for z in range(RING):
                    plane = (h * RING + source) * 16
                    pairs.append((plane + b * RING + z, plane + place((source - z) % RING, b ^ h, part)))
    return pairs


def shifted(part):
    pairs = []
    for h in range(2):
        for z in range(RING):
            for offset in range(RING):
                for other in range(2):
                    t = place(offset, other, part)
                    pairs.append(((h * RING + (z + offset) % RING) * 16 + t, (h * RING + z) * 16 + t))
    return pairs


def along_z(step):
    return [(h * RING + z, h * RING + (z + step) % RING) for h in range(2) for z in range(RING)]


ACROSS = [(i, (i + RING) % 16) for i in range(16)]


def product_body(low_ref, high_ref, columns_ref, out_ref, total):
    k = pl.program_id(0)
    low = low_ref.shape[3]
    high = out_ref.shape[0] - low

    def partial():
        return sum(
            lax.dot_general(
                jnp.concatenate([low_ref[0, 0, core], high_ref[0, 0, core, :high]]),
                columns_ref[core], (((1,), (1,)), ((), ())),
                preferred_element_type=jnp.float32,
            )
            for core in range(2)
        )

    @pl.when(k == 0)
    def _():
        total[...] = partial()

    @pl.when((k > 0) & (k < 3))
    def _():
        total[...] += partial()

    @pl.when(k == 3)
    def _():
        out_ref[...] = (total[...] + partial()).astype(out_ref.dtype)


def product(rows, columns, other, second, size, kind):
    n, tokens = columns.shape[1:]
    count = n - 2 * size if second else 2 * size

    def part_spec(part):
        return pl.BlockSpec((1, 1, 2, size, tokens), lambda k: ((k + part) & 3, other, 0, part, 0))

    return pl.pallas_call(
        product_body,
        grid=(4,),
        in_specs=[
            part_spec(2 * second), part_spec(2 * second + 1),
            pl.BlockSpec((2, n, tokens), lambda k: (k, 0, 0)),
        ],
        out_specs=pl.BlockSpec((count, n), lambda k: (0, 0)),
        out_shape=jax.ShapeDtypeStruct((count, n), kind),
        scratch_shapes=[pltpu.VMEM((count, n), jnp.float32)],
        compiler_params=pltpu.CompilerParams(
            dimension_semantics=("arbitrary",), vmem_limit_bytes=56 * 1024 * 1024
        ),
        cost_estimate=pl.CostEstimate(
            flops=2 * count * n * tokens * RING, bytes_accessed=12 * 1024 * 1024, transcendentals=0
        ),
    )(rows, rows, columns)


def put(columns, block, offset, start=0):
    return lax.dynamic_update_slice(columns, block[None], (PLACES.index(offset), start, 0))


def shards(out_grad, down_weight, gate_pre):
    n, tokens = down_weight.shape[0], out_grad.shape[0]
    size = -(-n // (16 * PARTS)) * 16
    cut = 2 * size
    hidden_grad = lax.dot_general(
        down_weight, out_grad, (((1,), (1,)), ((), ())), preferred_element_type=jnp.float32
    ).astype(jnp.bfloat16)
    up_grad = (hidden_grad.astype(jnp.float32) * jax.nn.silu(gate_pre.T.astype(jnp.float32))).astype(
        jnp.bfloat16
    )
    parts = [
        lax.ppermute(
            lax.ppermute(up_grad[part * size : (part + 1) * size], BOTH, in_plane(part)), BOTH, shifted(part)
        )
        for part in range(PARTS)
    ]
    rows, up_grad = lax.optimization_barrier((jnp.concatenate(parts), up_grad))
    rows = lax.all_gather(rows, "tensor", axis=0).reshape(4, 2, 2, n, tokens)

    columns = jnp.broadcast_to(up_grad[None], (RING, n, tokens))
    up, down = up_grad, up_grad
    for step in range(1, RING // 2):
        up, down = lax.ppermute(up, "dp", along_z(1)), lax.ppermute(down, "dp", along_z(-1))
        columns = put(put(columns, up, RING - step), down, step)
    up = lax.ppermute(up[:cut], "dp", along_z(1))
    down = lax.ppermute(down[cut:], "dp", along_z(-1))
    columns = put(put(columns, up, RING // 2), down, RING // 2, cut)

    total = tokens * lax.axis_size("dp")
    theirs = [
        product(rows, columns, 1, second, size, jnp.bfloat16).reshape(-1, 16, n) for second in range(2)
    ]
    sent = [lax.ppermute(part, "dp", ACROSS) for part in theirs]
    out = jnp.zeros((n, n), jnp.float32)
    for second in (1, 0):
        ours = product(rows, columns, 0, second, size, jnp.float32)
        part = (ours + sent[second].reshape(-1, n).astype(jnp.float32)) * (1.0 / total)
        out = lax.dynamic_update_slice(lax.optimization_barrier(out), part, (second * cut, 0))
    return out


def solution(mesh):
    placed = (P("dp", None), P("tensor", None), P("dp", "tensor"))
    return jax.shard_map(
        shards, mesh=mesh, in_specs=placed, out_specs=P("dp", "tensor"), check_vma=False
    )
```

```python
import jax
import jax.numpy as jnp
from jax import lax
from jax.experimental import pallas as pl
from jax.experimental.pallas import tpu as pltpu
from jax.sharding import PartitionSpec as P

BOTH = ("dp", "tensor")
RING = 8
PARTS = 4
PLACES = (0, 4, 1, 7, 2, 6, 3, 5)


def place(offset, other, part):
    pair, core = divmod(PLACES.index(offset), 2)
    return (pair + part) % 4 * 4 + other * 2 + core


def in_plane(part):
    pairs = []
    for h in range(2):
        for source in range(RING):
            for b in range(2):
                for z in range(RING):
                    plane = (h * RING + source) * 16
                    pairs.append((plane + b * RING + z, plane + place((source - z) % RING, b ^ h, part)))
    return pairs


def shifted(part):
    pairs = []
    for h in range(2):
        for z in range(RING):
            for offset in range(RING):
                for other in range(2):
                    t = place(offset, other, part)
                    pairs.append(((h * RING + (z + offset) % RING) * 16 + t, (h * RING + z) * 16 + t))
    return pairs


def along_z(step):
    return [(h * RING + z, h * RING + (z + step) % RING) for h in range(2) for z in range(RING)]


ACROSS = [(i, (i + RING) % 16) for i in range(16)]


def product_body(low_ref, high_ref, columns_ref, out_ref, total):
    k = pl.program_id(0)
    low = low_ref.shape[3]
    high = out_ref.shape[0] - low

    def partial():
        return sum(
            lax.dot_general(
                jnp.concatenate([low_ref[0, 0, core], high_ref[0, 0, core, :high]]),
                columns_ref[core], (((1,), (1,)), ((), ())),
                preferred_element_type=jnp.float32,
            )
            for core in range(2)
        )

    @pl.when(k == 0)
    def _():
        total[...] = partial()

    @pl.when((k > 0) & (k < 3))
    def _():
        total[...] += partial()

    @pl.when(k == 3)
    def _():
        out_ref[...] = (total[...] + partial()).astype(out_ref.dtype)


def product(rows, columns, other, second, size, kind):
    n, tokens = columns.shape[1:]
    count = n - 2 * size if second else 2 * size

    def part_spec(part):
        return pl.BlockSpec((1, 1, 2, size, tokens), lambda k: ((k + part) & 3, other, 0, part, 0))

    return pl.pallas_call(
        product_body,
        grid=(4,),
        in_specs=[
            part_spec(2 * second), part_spec(2 * second + 1),
            pl.BlockSpec((2, n, tokens), lambda k: (k, 0, 0)),
        ],
        out_specs=pl.BlockSpec((count, n), lambda k: (0, 0)),
        out_shape=jax.ShapeDtypeStruct((count, n), kind),
        scratch_shapes=[pltpu.VMEM((count, n), jnp.float32)],
        compiler_params=pltpu.CompilerParams(
            dimension_semantics=("arbitrary",), vmem_limit_bytes=56 * 1024 * 1024
        ),
        cost_estimate=pl.CostEstimate(
            flops=2 * count * n * tokens * RING, bytes_accessed=12 * 1024 * 1024, transcendentals=0
        ),
    )(rows, rows, columns)


def put(columns, block, offset, start=0):
    return lax.dynamic_update_slice(columns, block[None], (PLACES.index(offset), start, 0))


def shards(out_grad, down_weight, gate_pre):
    n, tokens = down_weight.shape[0], out_grad.shape[0]
    size = -(-n // (16 * PARTS)) * 16
    cut = 2 * size
    size = -(-n // (16 * PARTS)) * 16
    cut = 2 * size

    def some_units(low, high):
        hidden_grad = lax.dot_general(
            down_weight[low:high], out_grad, (((1,), (1,)), ((), ())), preferred_element_type=jnp.float32
        ).astype(jnp.bfloat16)
        gate = gate_pre[:, low:high].T.astype(jnp.float32)
        return (hidden_grad.astype(jnp.float32) * jax.nn.silu(gate)).astype(jnp.bfloat16)

    pieces = [some_units(0, cut), some_units(cut, n)]
    up_grad = jnp.concatenate(pieces)
    hidden_grad = lax.dot_general(
        down_weight, out_grad, (((1,), (1,)), ((), ())), preferred_element_type=jnp.float32
    ).astype(jnp.bfloat16)
    up_grad = (hidden_grad.astype(jnp.float32) * jax.nn.silu(gate_pre.T.astype(jnp.float32))).astype(
        jnp.bfloat16
    )
    parts = [
        lax.ppermute(
            lax.ppermute(pieces[part // 2][part % 2 * size : (part % 2 + 1) * size], BOTH, in_plane(part)), BOTH, shifted(part)
        )
        for part in range(PARTS)
    ]
    rows, up_grad = lax.optimization_barrier((jnp.concatenate(parts), up_grad))
    rows = lax.all_gather(rows, "tensor", axis=0).reshape(4, 2, 2, n, tokens)

    columns = jnp.broadcast_to(up_grad[None], (RING, n, tokens))
    up, down = up_grad, up_grad
    for step in range(1, RING // 2):
        up, down = lax.ppermute(up, "dp", along_z(1)), lax.ppermute(down, "dp", along_z(-1))
        columns = put(put(columns, up, RING - step), down, step)
    up = lax.ppermute(up[:cut], "dp", along_z(1))
    down = lax.ppermute(down[cut:], "dp", along_z(-1))
    columns = put(put(columns, up, RING // 2), down, RING // 2, cut)

    total = tokens * lax.axis_size("dp")
    theirs = [
        product(rows, columns, 1, second, size, jnp.bfloat16).reshape(-1, 16, n) for second in range(2)
    ]
    sent = [lax.ppermute(part, "dp", ACROSS) for part in theirs]
    out = jnp.zeros((n, n), jnp.float32)
    for second in (1, 0):
        ours = product(rows, columns, 0, second, size, jnp.float32)
        part = (ours + sent[second].reshape(-1, n).astype(jnp.float32)) * (1.0 / total)
        out = lax.dynamic_update_slice(lax.optimization_barrier(out), part, (second * cut, 0))
    return out


def solution(mesh):
    placed = (P("dp", None), P("tensor", None), P("dp", "tensor"))
    return jax.shard_map(
        shards, mesh=mesh, in_specs=placed, out_specs=P("dp", "tensor"), check_vma=False
    )
```
